512 devices in a mesh: group: 4 (over z_hi), seq: 8 (over x, z_lo), tp: 16 (over y, core).
Axes of the slice: x: 4, y: 8, z: 8 (z_hi: 4, z_lo: 2; z = z_hi * 2 + z_lo), core: 2. Of those that a mesh axis runs over, the one named last changes fastest.
Arguments:
- hidden: bfloat16 [4, 3072, 8192], P('group', 'seq', 'tp')
- passage_queries: bfloat16 [4, 3072, 8192], P('group', 'seq', 'tp')
- key_weight: bfloat16 [8192, 1024], P('tp'), may hold values from -0.0625 to 0.0625
- value_weight: bfloat16 [8192, 1024], P('tp'), may hold values from -0.0625 to 0.0625
- decode_queries: bfloat16 [4, 64, 8192], P(None, ('group', 'seq'))
- new_keys: bfloat16 [4, 64, 1024], P(None, ('group', 'seq')), may hold values from -9 to 9
- new_values: bfloat16 [4, 64, 1024], P(None, ('group', 'seq')), may hold values from -6 to 6
- cache_keys: bfloat16 [64, 2048, 1024], P(('group', 'seq'), 'tp'), may hold values from -6 to 6
- cache_values: bfloat16 [64, 2048, 1024], P(('group', 'seq'), 'tp'), may hold values from -6 to 6
- cache_lengths: int32 [64], P(('group', 'seq')), may hold values from 1 to 2048
- passage_of_row: int32 [64], P(('group', 'seq')), may hold values from 0 to 3
Outputs:
- passage_context: bfloat16 [4, 3072, 8192], P('group', 'seq', 'tp')
- row_context: bfloat16 [4, 64, 8192], P(None, ('group', 'seq'), 'tp')
The draws below stay inside these ranges and needn't reach their ends.
All inputs are finite; a program needn't handle non-finite values.
Results may differ from the reference program's by a relative error of at most 0.03.
Values may be sent and summed in bfloat16 or wider, within the bound.
No kernel may reach another device: no remote copies, remote signals or barrier semaphores. Data moves between devices by JAX's collectives and lax.ppermute only.
A program may use at most 64 MiB of HBM per device.

```python
from functools import partial
import jax
import jax.numpy as jnp
from jax import lax

D = 8192
QH = 64
KVH = 8
HS = 128
CACHE = 2048
STEPS = 4
NPASS = 4
PASSAGE = 3072
ROWS = 64


def draw_hidden(key, part):
    key = jax.random.fold_in(key, 7)
    entry_key, column_key, row_key = jax.random.split(key, 3)
    shape = (NPASS, PASSAGE, D)
    column_ramp = 10.0 ** (jnp.arange(D, dtype=jnp.float32) / (D - 1))
    columns = column_ramp * jnp.exp(0.3 * jax.random.normal(column_key, (D,), jnp.float32))
    row_scale = jnp.exp(jax.random.uniform(row_key, (NPASS, PASSAGE, 1), jnp.float32, 0.0, 2.3))
    entries = jax.random.normal(entry_key, shape, jnp.float32)
    return (entries * columns * row_scale).astype(jnp.bfloat16)


def draw_passage_queries(key, part):
    key = jax.random.fold_in(key, 21)
    entry_key = jax.random.fold_in(key, 0)
    shape = (NPASS, PASSAGE, QH * HS)
    entries = jax.random.normal(entry_key, shape, jnp.float32)
    return entries.astype(jnp.bfloat16)


def draw_decode_queries(key, part):
    key = jax.random.fold_in(key, 35)
    entry_key = jax.random.fold_in(key, 0)
    shape = (STEPS, ROWS, QH * HS)
    entries = 2.5 * jax.random.normal(entry_key, shape, jnp.float32)
    return entries.astype(jnp.bfloat16)


def touch_ends(array, stream_key, smallest, largest):
    longest = array.shape.index(max(array.shape))
    spots = []
    for shift in (0, 1):
        where = [jax.random.randint(jax.random.fold_in(stream_key, axis), (), 0, length) for axis, length in enumerate(array.shape)]
        where[longest] = (where[longest] + shift) % array.shape[longest]
        spots.append(tuple(where))
    return array.at[spots[0]].set(smallest).at[spots[1]].set(largest)


def level_of(rng, dims, shards, least, largest):
    factor_of = 1.0
    for axis_at, shards_of in shards:
        steps = jax.random.uniform(jax.random.fold_in(jax.random.fold_in(rng, 6), axis_at), (shards_of,), jnp.float32, least / len(shards), largest / len(shards))
        factor_of = factor_of * jnp.repeat(jnp.exp(steps), dims[axis_at] // shards_of).reshape((-1,) + (1,) * (len(dims) - 1 - axis_at))
    return factor_of


def normal_values(own_key, shape, deviation, reach, cuts=(), held_as=jnp.bfloat16):
    array = jax.random.normal(own_key, shape, jnp.float32) * deviation
    if len(cuts) > 0:
        array = level_of(own_key, shape, cuts, -0.22, 0.18) * array
    return jnp.clip(array, min=-reach, max=reach).astype(held_as)


def setup_inputs(seed: int = 0) -> dict:
    key_of = jax.random.split(jax.random.key(seed), 12)
    hidden = draw_hidden(jax.random.fold_in(key_of[11], 71), 0)
    passage_queries = draw_passage_queries(jax.random.fold_in(key_of[11], 71), 0)
    key_weight = normal_values(key_of[2], (D, KVH * HS), D ** -0.5, 0.0625, ((0, 16),))
    value_weight = normal_values(key_of[3], (D, KVH * HS), D ** -0.5, 0.0625, ((0, 16),))
    decode_queries = draw_decode_queries(jax.random.fold_in(key_of[11], 71), 0)
    new_keys = normal_values(key_of[5], (STEPS, ROWS, KVH * HS), 1.5, 9.0, ((1, 32),))
    new_values = normal_values(key_of[6], (STEPS, ROWS, KVH * HS), 1.0, 6.0, ((1, 32),))
    cache_keys = normal_values(key_of[7], (ROWS, CACHE, KVH * HS), 1.0, 6.0, ((0, 32), (1, 16)))
    cache_values = normal_values(key_of[8], (ROWS, CACHE, KVH * HS), 1.0, 6.0, ((0, 32), (1, 16)))
    cache_lengths = touch_ends(jax.random.randint(key_of[9], (ROWS,), 1, CACHE + 1), jax.random.fold_in(key_of[9], 1), 1, CACHE).astype(jnp.int32)
    passage_of_row = touch_ends(jax.random.randint(key_of[10], (ROWS,), 0, NPASS), jax.random.fold_in(key_of[10], 1), 0, NPASS - 1).astype(jnp.int32)
    return {"hidden": hidden, "passage_queries": passage_queries, "key_weight": key_weight, "value_weight": value_weight, "decode_queries": decode_queries, "new_keys": new_keys, "new_values": new_values, "cache_keys": cache_keys, "cache_values": cache_values, "cache_lengths": cache_lengths, "passage_of_row": passage_of_row}


ROPE_BASE = 500000.0
NORM_EPS = 1e-05
NEG_BIG = -1e+30

def rotate(values, positions):
    half_dim = values.shape[-1] // 2
    inv_freq = ROPE_BASE ** (-(jnp.arange(half_dim, dtype=jnp.float32) * 2.0 / values.shape[-1]))
    angles = positions.astype(jnp.float32)[:, None] * inv_freq[None, :]
    cosine = jnp.cos(angles)[:, None, :]
    sine_table = jnp.sin(angles)[:, None, :]
    lower_half = values[..., :half_dim]
    upper_half = values[..., half_dim:]
    return jnp.concatenate([lower_half * cosine - upper_half * sine_table, upper_half * cosine + lower_half * sine_table], axis=-1)

def attend(scores, allowed, value_head):
    highest = lax.optimization_barrier(jnp.max(jnp.where(allowed, scores, NEG_BIG), axis=-1, keepdims=True))
    exp_scores = jnp.where(allowed, jnp.exp(scores - highest), 0.0)
    weights = exp_scores.astype(jnp.bfloat16)
    totals = lax.optimization_barrier(jnp.sum(exp_scores, axis=-1, keepdims=True))
    return jnp.dot(weights, value_head, preferred_element_type=jnp.float32) / totals

def prefill_passage(inputs, key_weight, value_weight):
    states, queries = inputs
    widened = states.astype(jnp.float32)
    inverse = lax.rsqrt(lax.optimization_barrier(jnp.mean(widened * widened, axis=-1, keepdims=True)) + NORM_EPS)
    normed = (widened * inverse).astype(jnp.bfloat16)
    positions = jnp.arange(PASSAGE, dtype=jnp.int32)
    key_rows = jnp.dot(normed, key_weight, preferred_element_type=jnp.float32).reshape(PASSAGE, KVH, HS)
    key_rows = rotate(key_rows, positions).astype(jnp.bfloat16)
    value_rows = jnp.dot(normed, value_weight, preferred_element_type=jnp.float32).astype(jnp.bfloat16).reshape(PASSAGE, KVH, HS)
    turned = rotate(queries.astype(jnp.float32).reshape(PASSAGE, QH, HS), positions).astype(jnp.bfloat16)
    allowed = positions[:, None] >= positions[None, :]

    def head_context(head):
        kv_head = head // (QH // KVH)
        query_head = lax.dynamic_index_in_dim(turned, head, 1, keepdims=False)
        key_head = lax.dynamic_index_in_dim(key_rows, kv_head, 1, keepdims=False)
        value_head = lax.dynamic_index_in_dim(value_rows, kv_head, 1, keepdims=False)
        scores = jnp.dot(query_head, key_head.T, preferred_element_type=jnp.float32) * HS ** (-0.5)
        return attend(scores, allowed, value_head)
    contexts = lax.map(head_context, jnp.arange(QH, dtype=jnp.int32))
    context = jnp.transpose(contexts, (1, 0, 2)).reshape(PASSAGE, QH * HS).astype(jnp.bfloat16)
    return (context, key_rows, value_rows)

def reference(hidden, passage_queries, key_weight, value_weight, decode_queries, new_keys, new_values, cache_keys, cache_values, cache_lengths, passage_of_row):
    passage_context, all_keys, all_values = lax.map(partial(prefill_passage, key_weight=key_weight, value_weight=value_weight), (hidden, passage_queries))
    slot_ids = jnp.arange(CACHE, dtype=jnp.int32)
    step_ids = jnp.arange(STEPS, dtype=jnp.int32)

    def row_output(row):
        passage = passage_of_row[row]
        key_rows = jnp.concatenate([all_keys[passage], cache_keys[row].reshape(CACHE, KVH, HS), new_keys[:, row].reshape(STEPS, KVH, HS)], axis=0)
        value_rows = jnp.concatenate([all_values[passage], cache_values[row].reshape(CACHE, KVH, HS), new_values[:, row].reshape(STEPS, KVH, HS)], axis=0)
        allowed = jnp.concatenate([jnp.ones((STEPS, PASSAGE), dtype=bool), jnp.broadcast_to(slot_ids[None, :] < cache_lengths[row], (STEPS, CACHE)), step_ids[None, :] <= step_ids[:, None]], axis=1)[:, None, None, :]
        queries = decode_queries[:, row].reshape(STEPS, KVH, QH // KVH, HS).astype(jnp.float32)
        scores = jnp.einsum('skgh,nkh->skgn', queries, key_rows.astype(jnp.float32)) * HS ** (-0.5)
        highest = lax.optimization_barrier(jnp.max(jnp.where(allowed, scores, NEG_BIG), axis=-1, keepdims=True))
        exp_scores = jnp.where(allowed, jnp.exp(scores - highest), 0.0)
        weights = lax.optimization_barrier(exp_scores.astype(jnp.bfloat16)).astype(jnp.float32)
        totals = lax.optimization_barrier(jnp.sum(exp_scores, axis=-1))
        context = jnp.einsum('skgn,nkh->skgh', weights, value_rows.astype(jnp.float32)) / totals[..., None]
        return context.reshape(STEPS, QH * HS)
    rows_out = lax.map(row_output, jnp.arange(ROWS, dtype=jnp.int32))
    row_context = jnp.transpose(rows_out, (1, 0, 2)).astype(jnp.bfloat16)
    return (passage_context, row_context)
```

```python
import functools

import jax
import jax.numpy as jnp
import numpy as np
from jax import lax
from jax.experimental import pallas as pl
from jax.experimental.pallas import tpu as pltpu
from jax.sharding import Mesh
from jax.sharding import PartitionSpec as P

D = 8192
KVH = 8
HS = 128
SEQ = 8
TOK = 384
HALF = 192
HEADS = 4
EXTRA = 16
STATE = 40
ROPE_BASE = 500000.0
NORM_EPS = 1e-05
NEG = -1e30
SCALE2 = float(HS**-0.5 * np.log2(np.e))

bf16, f32 = jnp.bfloat16, jnp.float32
dot = functools.partial(jnp.dot, preferred_element_type=f32)


def dot_t(a, b):
    return lax.dot_general(a, b, (((1,), (1,)), ((), ())), preferred_element_type=f32)


def tables():
    freq = ROPE_BASE ** (-(np.arange(HS // 2) * 2.0 / HS))
    freq = np.concatenate([freq, freq])
    near = np.arange(TOK)[:, None] * freq
    far = (np.arange(SEQ) * TOK)[:, None] * freq
    near = np.stack([np.cos(near), np.sin(near)]).astype(np.float32)
    far = np.stack([np.cos(far), np.sin(far)]).astype(np.float32)
    return near, far


def turn_by(near_ref, far_ref, s, rows):
    cn, sn = near_ref[0, rows, :], near_ref[1, rows, :]
    cf, sf = far_ref[0, pl.ds(s, 1), :], far_ref[1, pl.ds(s, 1), :]
    cosine = cn * cf - sn * sf
    sine = sn * cf + cn * sf
    lane = lax.broadcasted_iota(jnp.int32, sine.shape, 1)
    return cosine, jnp.where(lane < HS // 2, -sine, sine)


def turned(x, cosine, sine):
    return x * cosine + pltpu.roll(x, HS // 2, 1) * sine


def project(mine, where_ref, hidden_ref, key_ref, value_ref, out_ref, squares_ref):
    core = where_ref[1] if mine else 1 - where_ref[1]
    rows = pl.ds(pl.multiple_of(core * HALF, HALF), HALF)

    @pl.when(pl.program_id(0) == 0)
    def _():
        h = hidden_ref[rows, :].astype(f32)
        sq = h * h
        high = sq.astype(bf16)
        low = (sq - high.astype(f32)).astype(bf16)
        ones = jnp.ones((EXTRA, hidden_ref.shape[1]), bf16)
        sums = dot_t(ones, high) + dot_t(ones, low)
        sums = jnp.concatenate([sums, jnp.zeros((EXTRA, 256 - HALF), f32)], axis=1)
        row = lax.broadcasted_iota(jnp.int32, (EXTRA, 256), 0)
        squares_ref[...] = jnp.where(row == where_ref[2], sums, 0.0).astype(bf16)

    h = hidden_ref[rows, :]
    keys = dot(h, key_ref[...]).astype(bf16)
    values = dot(h, value_ref[...]).astype(bf16)
    for j in range(out_ref.shape[0]):
        out_ref[j, :HALF, :HS] = keys[:, j * HS : (j + 1) * HS]
        out_ref[j, :HALF, HS:] = values[:, j * HS : (j + 1) * HS]
        out_ref[j, HALF:, :] = squares_ref[...]


def add(mine_ref, other_ref, out_ref):
    out_ref[...] = (mine_ref[...].astype(f32) + other_ref[...].astype(f32)).astype(bf16)


def finish_share(where_ref, sums_ref, near_ref, far_ref, out_ref):
    s, core = where_ref[0], where_ref[1]
    squares, sums = 0.0, 0.0
    for k in range(sums_ref.shape[0]):
        sums = sums + sums_ref[k, :HALF, :].astype(f32)
        squares = squares + sums_ref[k, HALF:, :].astype(f32)
    squares = jnp.sum(squares, axis=0, keepdims=True)
    inverse = lax.rsqrt(squares * (1.0 / D) + NORM_EPS)
    inverse = jnp.transpose(jnp.broadcast_to(inverse, (8, 256)))[:HALF, 0:1]
    alive = inverse > 0.0
    scaled = jnp.where(alive, sums * inverse, 0.0)
    rows = pl.ds(pl.multiple_of(core * HALF, HALF), HALF)
    cosine, sine = turn_by(near_ref, far_ref, s, rows)
    keys = turned(scaled[:, :HS], cosine, sine)
    share = jnp.concatenate([keys, scaled[:, HS:]], axis=1).astype(bf16)
    for to in range(SEQ):
        out_ref[to] = share


def put_state(out_ref, at, weighted, highest, totals):
    rows = weighted.shape[0]
    lane = lax.broadcasted_iota(jnp.int32, (rows, HS), 1)
    both = jnp.where(lane == 0, highest, jnp.where(lane == 1, totals, 0.0))
    flat = jnp.transpose(both)[:8, :]
    for j in range(rows // 32):
        out_ref[at + j, :32, :] = weighted[j * 32 : (j + 1) * 32, :]
        out_ref[at + j, 32:, :] = jnp.concatenate(
            [flat[:, j * 32 : (j + 1) * 32], jnp.zeros((8, HS - 32), f32)], axis=1
        )


def cache_states(
    where_ref, length_ref, query_ref, new_ref, key_ref, value_ref, out_ref
):
    tp = where_ref[2]
    slots = key_ref.shape[1]
    rows = 64
    q = lax.broadcasted_iota(jnp.int32, (rows, 2 * slots), 0)
    n = lax.broadcasted_iota(jnp.int32, (rows, 2 * slots), 1)
    key_row = jnp.where(n >= slots, 1, 0)
    slot = tp * slots + n - key_row * slots
    length = jnp.where(key_row == 1, length_ref[1], length_ref[0])
    live = ((q & 1) == key_row) & (slot < length)
    q = lax.broadcasted_iota(jnp.int32, (rows, 8), 0)
    n = lax.broadcasted_iota(jnp.int32, (rows, 8), 1)
    recent = ((q & 1) == (n & 1)) & ((n & 7) >> 1 <= (q & 7) >> 1) & (tp == 0)
    for head in range(KVH):
        cols = slice(head * HS, (head + 1) * HS)
        query = jnp.concatenate(
            [query_ref[:, (head * 8 + p) * HS : (head * 8 + p + 1) * HS] for p in range(8)], axis=0
        )
        low = query.astype(bf16)
        keys = jnp.concatenate([key_ref[0, :, cols], key_ref[1, :, cols]], axis=0)
        values = jnp.concatenate([value_ref[0, :, cols], value_ref[1, :, cols]], axis=0)
        new_keys = new_ref[:, cols].astype(bf16)
        new_values = new_ref[:, KVH * HS + head * HS : KVH * HS + (head + 1) * HS].astype(bf16)
        scores = jnp.where(live, dot_t(low, keys) * SCALE2, NEG)
        news = jnp.where(recent, dot_t(low, new_keys) * SCALE2, NEG)
        highest = jnp.maximum(
            jnp.max(scores, axis=1, keepdims=True), jnp.max(news, axis=1, keepdims=True)
        )
        weights = jnp.where(live, jnp.exp2(scores - highest), 0.0)
        new_weights = jnp.where(recent, jnp.exp2(news - highest), 0.0)
        totals = jnp.sum(weights, axis=1, keepdims=True) + jnp.sum(
            new_weights, axis=1, keepdims=True
        )
        weighted = dot(weights.astype(bf16), values) + dot(new_weights.astype(bf16), new_values)
        put_state(out_ref, 2 * head, weighted, highest, totals)


def passage_states(query_ref, own_ref, other_ref, out_ref):
    query = jnp.concatenate(
        [
            query_ref[g, :, p * HS : (p + 1) * HS]
            for g in range(query_ref.shape[0])
            for p in range(HEADS)
        ],
        axis=0,
    ).astype(bf16)
    refs = (own_ref, other_ref)
    scores = [dot_t(query, ref[:, :HS]) * SCALE2 for ref in refs]
    highest = jnp.max(jnp.maximum(*scores), axis=1, keepdims=True)
    weights = [jnp.exp2(score - highest) for score in scores]
    totals = jnp.sum(weights[0] + weights[1], axis=1, keepdims=True)
    weighted = sum(dot(w.astype(bf16), ref[:, HS:]) for w, ref in zip(weights, refs, strict=True))
    put_state(out_ref, 0, weighted, highest, totals)


def attend(
    where_ref,
    query_ref,
    near_ref,
    far_ref,
    own_ref,
    other_ref,
    out_ref,
    high_ref,
    sum_ref,
    turned_ref,
):
    s, core = where_ref[0], where_ref[1]
    cosine, sine = turn_by(near_ref, far_ref, s, slice(None))
    for h in range(HEADS):
        x = query_ref[:, h * HS : (h + 1) * HS].astype(f32)
        turned_ref[h] = turned(x, cosine, sine).astype(bf16)
    ones = jnp.ones((TOK, HS), bf16)
    last = s // 2

    def blocks(pair):
        at = pl.multiple_of(pair * TOK, TOK)
        return [ref[pl.ds(at, TOK), :] for ref in (own_ref, other_ref)]

    def weigh(scores, highest, kv):
        total = 0.0
        for score, block in zip(scores, kv, strict=True):
            weights = jnp.exp2(score * SCALE2 - highest * SCALE2).astype(bf16)
            total = total + dot(weights, jnp.concatenate([block[:, HS:], ones], axis=1))
        return total

    kv = blocks(last)
    query_pos = s * TOK + lax.broadcasted_iota(jnp.int32, (TOK, TOK), 0)
    n = lax.broadcasted_iota(jnp.int32, (TOK, TOK), 1)
    second = jnp.where(n >= HALF, 1, 0)
    key_pos = (2 * last + second) * TOK + n - second * HALF
    allowed = [key_pos + c * HALF <= query_pos for c in (core, 1 - core)]
    for h in range(HEADS):
        query = turned_ref[h]
        scores = [
            jnp.where(ok, dot_t(query, block[:, :HS]), NEG)
            for ok, block in zip(allowed, kv, strict=True)
        ]
        highest = jnp.max(jnp.maximum(scores[0], scores[1]), axis=1, keepdims=True)
        high_ref[h] = jnp.broadcast_to(highest, (TOK, HS))
        sum_ref[h] = weigh(scores, highest, kv)

    def step(i, carry):
        kv = blocks(last - 1 - i)
        for h in range(HEADS):
            query = turned_ref[h]
            scores = [dot_t(query, block[:, :HS]) for block in kv]
            before = high_ref[h, :, 0:1]
            highest = jnp.maximum(
                before, jnp.max(jnp.maximum(scores[0], scores[1]), axis=1, keepdims=True)
            )
            factor = jnp.exp2((before - highest) * SCALE2)
            high_ref[h] = jnp.broadcast_to(highest, (TOK, HS))
            sum_ref[h] = sum_ref[h] * factor + weigh(scores, highest, kv)
        return carry

    lax.fori_loop(0, last, step, 0)
    for h in range(HEADS):
        out_ref[:, h * HS : (h + 1) * HS] = (
            sum_ref[h, :, :HS] / sum_ref[h, :, HS : HS + 1]
        ).astype(bf16)


def merge(passage_ref, passages_ref, caches_ref, out_ref):
    count, sources = passages_ref.shape[0], caches_ref.shape[0]
    tail = jnp.transpose(caches_ref[:, 32:, :].reshape(sources * 8, HS))[:32, :]
    row = lax.broadcasted_iota(jnp.int32, (32, 1), 0) & 1
    chosen = jnp.where(row == 1, passage_ref[1], passage_ref[0])
    tails = jnp.concatenate(
        [passages_ref[:, 32:, :].reshape(count * 8, HS), jnp.zeros((HS - count * 8, HS), f32)],
        axis=0,
    )
    tails = jnp.transpose(tails)[:32, :]
    highs = [tail[:, 8 * t : 8 * t + 1] for t in range(sources)]
    totals = [tail[:, 8 * t + 1 : 8 * t + 2] for t in range(sources)]
    states = [caches_ref[t, :32, :] for t in range(sources)]
    high, total, state = tails[:, 0:1], tails[:, 1:2], passages_ref[0, :32, :]
    for g in range(1, count):
        high = jnp.where(chosen == g, tails[:, 8 * g : 8 * g + 1], high)
        total = jnp.where(chosen == g, tails[:, 8 * g + 1 : 8 * g + 2], total)
        state = jnp.where(chosen == g, passages_ref[g, :32, :], state)
    highest = functools.reduce(jnp.maximum, highs, high)
    factor = jnp.exp2(high - highest)
    total, state = total * factor, state * factor
    for t in range(sources):
        factor = jnp.exp2(highs[t] - highest)
        total = total + totals[t] * factor
        state = state + states[t] * factor
    context = state / total
    for p in range(HEADS):
        out_ref[:, p * HS : (p + 1) * HS] = context[p * 8 : (p + 1) * 8, :]


def vmem(count):
    return [pl.BlockSpec(memory_space=pltpu.VMEM)] * count


def smem(count):
    return [pl.BlockSpec(memory_space=pltpu.SMEM)] * count


def params(mib):
    return pltpu.CompilerParams(vmem_limit_bytes=mib << 20)


def cost(flops, transcendentals=0, bytes_accessed=1 << 20):
    return pl.CostEstimate(
        flops=flops, transcendentals=transcendentals, bytes_accessed=bytes_accessed
    )


def per_device(
    hidden,
    passage_queries,
    key_weight,
    value_weight,
    decode_queries,
    new_keys,
    new_values,
    cache_keys,
    cache_values,
    cache_lengths,
    passage_of_row,
):
    near, far = tables()
    core, y, s = lax.axis_index("core"), lax.axis_index("y"), lax.axis_index("seq")
    groups = lax.axis_size("group")
    tp = y * 2 + core
    where = jnp.stack([s, core, tp, tp]).astype(jnp.int32)
    features = hidden.shape[2]

    with jax.named_scope("decode_query_exchange"):
        queries = decode_queries.reshape(8, -1).astype(f32)
        own = lax.dynamic_slice_in_dim(queries, tp * HEADS * HS, HEADS * HS, 1)
        own = jnp.broadcast_to(own[None], (groups, 8, HEADS * HS))
        group_queries = lax.all_to_all(own, "group", 0, 0, tiled=True)

    swap = [(0, 1), (1, 0)]
    with jax.named_scope("projection"):
        width = 2

        def projected(mine):
            return pl.pallas_call(
                functools.partial(project, mine),
                grid=(KVH // width,),
                in_specs=smem(1)
                + [
                    pl.BlockSpec((TOK, features), lambda i: (0, 0)),
                    pl.BlockSpec((features, width * HS), lambda i: (0, i)),
                    pl.BlockSpec((features, width * HS), lambda i: (0, i)),
                ],
                out_specs=pl.BlockSpec((width, HALF + EXTRA, 2 * HS), lambda i: (i, 0, 0)),
                out_shape=jax.ShapeDtypeStruct((KVH, HALF + EXTRA, 2 * HS), bf16),
                scratch_shapes=[pltpu.VMEM((EXTRA, 256), bf16)],
                compiler_params=params(56),
                cost_estimate=cost(TOK * features * 2048, 0, 4 << 20),
            )(where, hidden[0], key_weight, value_weight)

        theirs = lax.ppermute(projected(False), "core", swap)
        chunks = pl.pallas_call(
            add,
            in_specs=vmem(2),
            out_specs=vmem(1)[0],
            out_shape=jax.ShapeDtypeStruct((KVH, HALF + EXTRA, 2 * HS), bf16),
            compiler_params=params(32),
            cost_estimate=cost(1 << 20),
        )(projected(True), theirs)
        sums = lax.all_to_all(chunks, "y", 0, 0, tiled=True)

    with jax.named_scope("share"):
        share = pl.pallas_call(
            finish_share,
            in_specs=smem(1) + vmem(3),
            out_specs=vmem(1)[0],
            out_shape=jax.ShapeDtypeStruct((SEQ, HALF, 2 * HS), bf16),
            compiler_params=params(32),
            cost_estimate=cost(1 << 20),
        )(where, sums, near, far)
        received = lax.all_to_all(share, "seq", 0, 0, tiled=True)

    with jax.named_scope("cache"):
        news = jnp.concatenate([new_keys, new_values], axis=2).reshape(8, -1).astype(f32)
        news, queries, _ = lax.optimization_barrier((news, queries, chunks))
        cached = pl.pallas_call(
            cache_states,
            in_specs=smem(2) + vmem(4),
            out_specs=vmem(1)[0],
            out_shape=jax.ShapeDtypeStruct((16, STATE, HS), f32),
            compiler_params=params(32),
            cost_estimate=cost(8 * 64 * 256 * 128 * 4, 8 * 64 * 256, 2 << 20),
        )(where, cache_lengths, queries, news, cache_keys, cache_values)
        cached, _ = lax.optimization_barrier((cached, share))
        cached = lax.all_to_all(cached, ("y", "core"), 0, 0, tiled=True)

    with jax.named_scope("passage_rows"):
        own_kv = received.reshape(SEQ * HALF, 2 * HS)
        other_kv = lax.ppermute(own_kv, "core", swap)
        rows_passage = pl.pallas_call(
            passage_states,
            in_specs=vmem(3),
            out_specs=vmem(1)[0],
            out_shape=jax.ShapeDtypeStruct((groups, STATE, HS), f32),
            compiler_params=params(32),
            cost_estimate=cost(128 * 3072 * 128 * 4, 128 * 3072, 2 << 20),
        )(group_queries, own_kv, other_kv)
        returned = lax.all_to_all(rows_passage, "group", 0, 0, tiled=True)

    with jax.named_scope("passage_attention"):
        passage_out = pl.pallas_call(
            attend,
            in_specs=smem(1) + vmem(5),
            out_specs=vmem(1)[0],
            out_shape=jax.ShapeDtypeStruct((TOK, HEADS * HS), bf16),
            scratch_shapes=[
                pltpu.VMEM((HEADS, TOK, HS), f32),
                pltpu.VMEM((HEADS, TOK, 2 * HS), f32),
                pltpu.VMEM((HEADS, TOK, HS), bf16),
            ],
            compiler_params=params(48),
            cost_estimate=cost(1536 * 3072 * 128 * 4 * 4, 1536 * 3072, 3 << 20),
        )(where, passage_queries[0], near, far, own_kv, other_kv)

    with jax.named_scope("row_merge"):
        row_out = pl.pallas_call(
            merge,
            in_specs=smem(1) + vmem(2),
            out_specs=vmem(1)[0],
            out_shape=jax.ShapeDtypeStruct((8, HEADS * HS), f32),
            compiler_params=params(32),
            cost_estimate=cost(1 << 20),
        )(passage_of_row, returned, cached)
    return passage_out[None], row_out.astype(bf16).reshape(4, 2, HEADS * HS)


def solution(mesh):
    shape = tuple(mesh.shape[name] for name in ("group", "seq", "tp"))
    split = Mesh(
        mesh.devices.reshape(shape[0], shape[1], shape[2] // 2, 2), ("group", "seq", "y", "core")
    )
    tp, rows = ("y", "core"), ("group", "seq")
    in_specs = (
        P("group", "seq", tp),
        P("group", "seq", tp),
        P(tp, None),
        P(tp, None),
        P(None, rows, None),
        P(None, rows, None),
        P(None, rows, None),
        P(rows, tp, None),
        P(rows, tp, None),
        P(rows),
        P(rows),
    )
    out_specs = (P("group", "seq", tp), P(None, rows, tp))
    return jax.shard_map(
        per_device, mesh=split, in_specs=in_specs, out_specs=out_specs, check_vma=False
    )
```

```python
import functools

import jax
import jax.numpy as jnp
import numpy as np
from jax import lax
from jax.experimental import pallas as pl
from jax.experimental.pallas import tpu as pltpu
from jax.sharding import Mesh
from jax.sharding import PartitionSpec as P

D = 8192
KVH = 8
HS = 128
SEQ = 8
TOK = 384
HALF = 192
HEADS = 4
EXTRA = 16
ROPE_BASE = 500000.0
NORM_EPS = 1e-05
NEG = -1e30
SCALE2 = float(HS**-0.5 * np.log2(np.e))

bf16, f32 = jnp.bfloat16, jnp.float32
dot = functools.partial(jnp.dot, preferred_element_type=f32)


def dot_t(a, b):
    return lax.dot_general(a, b, (((1,), (1,)), ((), ())), preferred_element_type=f32)


def tables():
    freq = ROPE_BASE ** (-(np.arange(HS // 2) * 2.0 / HS))
    freq = np.concatenate([freq, freq])
    near = np.arange(TOK)[:, None] * freq
    far = (np.arange(SEQ) * TOK)[:, None] * freq
    near = np.stack([np.cos(near), np.sin(near)]).astype(np.float32)
    far = np.stack([np.cos(far), np.sin(far)]).astype(np.float32)
    return near, far


def turn_by(near_ref, far_ref, s, rows):
    cn, sn = near_ref[0, rows, :], near_ref[1, rows, :]
    cf, sf = far_ref[0, pl.ds(s, 1), :], far_ref[1, pl.ds(s, 1), :]
    cosine = cn * cf - sn * sf
    sine = sn * cf + cn * sf
    lane = lax.broadcasted_iota(jnp.int32, sine.shape, 1)
    return cosine, jnp.where(lane < HS // 2, -sine, sine)


def turned(x, cosine, sine):
    return x * cosine + pltpu.roll(x, HS // 2, 1) * sine


def project(where_ref, hidden_ref, key_ref, value_ref, mine_ref, theirs_ref, squares_ref):
    core = where_ref[1]

    @pl.when(pl.program_id(0) == 0)
    def _():
        h = hidden_ref[...].astype(f32)
        sq = h * h
        high = sq.astype(bf16)
        low = (sq - high.astype(f32)).astype(bf16)
        ones = jnp.ones((EXTRA, hidden_ref.shape[1]), bf16)
        row = lax.broadcasted_iota(jnp.int32, (EXTRA, 256), 0)
        for half in range(2):
            part = slice(half * HALF, (half + 1) * HALF)
            sums = dot_t(ones, high[part]) + dot_t(ones, low[part])
            sums = jnp.concatenate([sums, jnp.zeros((EXTRA, 256 - HALF), f32)], axis=1)
            squares_ref[half] = jnp.where(row == where_ref[2], sums, 0.0).astype(bf16)

    h = hidden_ref[...]
    keys = dot(h, key_ref[...]).astype(bf16)
    values = dot(h, value_ref[...]).astype(bf16)

    def put(out_ref, half):
        part = slice(half * HALF, (half + 1) * HALF)
        for j in range(out_ref.shape[0]):
            out_ref[j, :HALF, :HS] = keys[part, j * HS : (j + 1) * HS]
            out_ref[j, :HALF, HS:] = values[part, j * HS : (j + 1) * HS]
            out_ref[j, HALF:, :] = squares_ref[half]

    @pl.when(core == 0)
    def _():
        put(mine_ref, 0)
        put(theirs_ref, 1)

    @pl.when(core == 1)
    def _():
        put(mine_ref, 1)
        put(theirs_ref, 0)


def add(mine_ref, other_ref, out_ref):
    out_ref[...] = (mine_ref[...].astype(f32) + other_ref[...].astype(f32)).astype(bf16)


def finish_share(where_ref, sums_ref, near_ref, far_ref, before_a, before_b, out_ref):
    del before_a, before_b
    s, core = where_ref[0], where_ref[1]
    squares, sums = 0.0, 0.0
    for k in range(sums_ref.shape[0]):
        sums = sums + sums_ref[k, :HALF, :].astype(f32)
        squares = squares + sums_ref[k, HALF:, :].astype(f32)
    squares = jnp.sum(squares, axis=0, keepdims=True)
    inverse = lax.rsqrt(squares * (1.0 / D) + NORM_EPS)
    inverse = jnp.transpose(jnp.broadcast_to(inverse, (8, 256)))[:HALF, 0:1]
    alive = inverse > 0.0
    scaled = jnp.where(alive, sums * inverse, 0.0)
    rows = pl.ds(pl.multiple_of(core * HALF, HALF), HALF)
    cosine, sine = turn_by(near_ref, far_ref, s, rows)
    keys = turned(scaled[:, :HS], cosine, sine)
    share = jnp.concatenate([keys, scaled[:, HS:]], axis=1).astype(bf16)
    for to in range(SEQ):
        out_ref[to] = share


def state_of(weighted, highest, totals):
    lane = lax.broadcasted_iota(jnp.int32, weighted.shape, weighted.ndim - 1)
    tail = jnp.where(lane < HS // 2, highest, totals)
    return jnp.concatenate([weighted, tail], axis=-1)


def parts_of(state):
    return state[..., :HS], state[..., HS : HS + 1], state[..., HS + HS // 2 : HS + HS // 2 + 1]


def merged(a, b):
    (a_sum, a_high, a_total), (b_sum, b_high, b_total) = parts_of(a), parts_of(b)
    highest = jnp.maximum(a_high, b_high)
    a_factor, b_factor = jnp.exp2(a_high - highest), jnp.exp2(b_high - highest)
    return state_of(
        a_sum * a_factor + b_sum * b_factor, highest, a_total * a_factor + b_total * b_factor
    )


def merge_halves(bit, where_ref, keep_ref, other_ref, out_ref, *send_ref):
    half = keep_ref.shape[0] // 2
    mine = (where_ref[3] >> bit) & 1
    keep, send = pl.ds(mine * half, half), pl.ds((1 - mine) * half, half)
    out_ref[...] = merged(keep_ref[keep], other_ref[keep])
    send_ref[0][...] = merged(keep_ref[send], other_ref[send])


def merge_last(keep_ref, other_ref, out_ref):
    out_ref[...] = merged(keep_ref[...], other_ref[...])


def cache_states(
    where_ref, length_ref, query_ref, new_ref, key_ref, value_ref, keep_ref, send_ref
):
    core, tp = where_ref[1], where_ref[2]
    slots = key_ref.shape[1]
    rows = 64
    q = lax.broadcasted_iota(jnp.int32, (rows, 2 * slots), 0)
    n = lax.broadcasted_iota(jnp.int32, (rows, 2 * slots), 1)
    key_row = jnp.where(n >= slots, 1, 0)
    slot = tp * slots + n - key_row * slots
    length = jnp.where(key_row == 1, length_ref[1], length_ref[0])
    live = ((q & 1) == key_row) & (slot < length)
    q = lax.broadcasted_iota(jnp.int32, (rows, 8), 0)
    n = lax.broadcasted_iota(jnp.int32, (rows, 8), 1)
    recent = ((q & 1) == (n & 1)) & ((n & 7) >> 1 <= (q & 7) >> 1) & (tp == 0)
    for head in range(KVH):
        cols = slice(head * HS, (head + 1) * HS)
        query = jnp.concatenate(
            [query_ref[:, (head * 8 + p) * HS : (head * 8 + p + 1) * HS] for p in range(8)], axis=0
        )
        low = query.astype(bf16)
        keys = jnp.concatenate([key_ref[0, :, cols], key_ref[1, :, cols]], axis=0)
        values = jnp.concatenate([value_ref[0, :, cols], value_ref[1, :, cols]], axis=0)
        new_keys = new_ref[:, cols].astype(bf16)
        new_values = new_ref[:, KVH * HS + head * HS : KVH * HS + (head + 1) * HS].astype(bf16)
        scores = jnp.where(live, dot_t(low, keys) * SCALE2, NEG)
        news = jnp.where(recent, dot_t(low, new_keys) * SCALE2, NEG)
        highest = jnp.maximum(
            jnp.max(scores, axis=1, keepdims=True), jnp.max(news, axis=1, keepdims=True)
        )
        weights = jnp.where(live, jnp.exp2(scores - highest), 0.0)
        new_weights = jnp.where(recent, jnp.exp2(news - highest), 0.0)
        totals = jnp.sum(weights, axis=1, keepdims=True) + jnp.sum(
            new_weights, axis=1, keepdims=True
        )
        weighted = dot(weights.astype(bf16), values) + dot(new_weights.astype(bf16), new_values)
        state = state_of(weighted, highest, totals)
        keep_ref[head] = jnp.where(core == 0, state[:32], state[32:])
        send_ref[head] = jnp.where(core == 0, state[32:], state[:32])


def passage_states(
    where_ref, query_ref, query1_ref, query2_ref, own_ref, other_ref, before, out_ref
):
    del before
    queries = [query_ref[...], query1_ref[...], query2_ref[:8, :], query2_ref[8:, :]]
    query = jnp.concatenate(
        [rows[:, p * HS : (p + 1) * HS] for rows in queries for p in range(HEADS)], axis=0
    ).astype(bf16)
    refs = (own_ref, other_ref)
    scores = [dot_t(query, ref[:, :HS]) * SCALE2 for ref in refs]
    highest = jnp.max(jnp.maximum(*scores), axis=1, keepdims=True)
    weights = [jnp.exp2(score - highest) for score in scores]
    totals = jnp.sum(weights[0] + weights[1], axis=1, keepdims=True)
    weighted = sum(dot(w.astype(bf16), ref[:, HS:]) for w, ref in zip(weights, refs, strict=True))
    state = state_of(weighted, highest, totals)
    for r in range(4):
        out_ref[where_ref[4] ^ r] = state[32 * r : 32 * (r + 1)]


def attend(
    where_ref,
    query_ref,
    near_ref,
    far_ref,
    own_ref,
    other_ref,
    out_ref,
    high_ref,
    sum_ref,
    turned_ref,
):
    s, core = where_ref[0], where_ref[1]
    cosine, sine = turn_by(near_ref, far_ref, s, slice(None))
    for h in range(HEADS):
        x = query_ref[:, h * HS : (h + 1) * HS].astype(f32)
        turned_ref[h] = turned(x, cosine, sine).astype(bf16)
    ones = jnp.ones((TOK, HS), bf16)
    last = s // 2

    def blocks(pair):
        at = pl.multiple_of(pair * TOK, TOK)
        return [ref[pl.ds(at, TOK), :] for ref in (own_ref, other_ref)]

    def weigh(scores, highest, kv):
        total = 0.0
        for score, block in zip(scores, kv, strict=True):
            weights = jnp.exp2(score * SCALE2 - highest * SCALE2).astype(bf16)
            total = total + dot(weights, jnp.concatenate([block[:, HS:], ones], axis=1))
        return total

    kv = blocks(last)
    query_pos = s * TOK + lax.broadcasted_iota(jnp.int32, (TOK, TOK), 0)
    n = lax.broadcasted_iota(jnp.int32, (TOK, TOK), 1)
    second = jnp.where(n >= HALF, 1, 0)
    key_pos = (2 * last + second) * TOK + n - second * HALF
    allowed = [key_pos + c * HALF <= query_pos for c in (core, 1 - core)]
    for h in range(HEADS):
        query = turned_ref[h]
        scores = [
            jnp.where(ok, dot_t(query, block[:, :HS]), NEG)
            for ok, block in zip(allowed, kv, strict=True)
        ]
        highest = jnp.max(jnp.maximum(scores[0], scores[1]), axis=1, keepdims=True)
        high_ref[h] = jnp.broadcast_to(highest, (TOK, HS))
        sum_ref[h] = weigh(scores, highest, kv)

    def step(i, carry):
        kv = blocks(last - 1 - i)
        for h in range(HEADS):
            query = turned_ref[h]
            scores = [dot_t(query, block[:, :HS]) for block in kv]
            before = high_ref[h, :, 0:1]
            highest = jnp.maximum(
                before, jnp.max(jnp.maximum(scores[0], scores[1]), axis=1, keepdims=True)
            )
            factor = jnp.exp2((before - highest) * SCALE2)
            high_ref[h] = jnp.broadcast_to(highest, (TOK, HS))
            sum_ref[h] = sum_ref[h] * factor + weigh(scores, highest, kv)
        return carry

    lax.fori_loop(0, last, step, 0)
    for h in range(HEADS):
        out_ref[:, h * HS : (h + 1) * HS] = (
            sum_ref[h, :, :HS] / sum_ref[h, :, HS : HS + 1]
        ).astype(bf16)


def merge(passage_ref, passages_ref, cache_ref, out_ref):
    row = lax.broadcasted_iota(jnp.int32, (32, 2 * HS), 0) & 1
    chosen = jnp.where(row == 1, passage_ref[1], passage_ref[0])
    state = passages_ref[0]
    for g in range(1, passages_ref.shape[0]):
        state = jnp.where(chosen == g, passages_ref[g], state)
    weighted, _, total = parts_of(merged(state, cache_ref[0]))
    context = weighted / total
    for p in range(HEADS):
        out_ref[:, p * HS : (p + 1) * HS] = context[p * 8 : (p + 1) * 8, :]


def vmem(count):
    return [pl.BlockSpec(memory_space=pltpu.VMEM)] * count


def smem(count):
    return [pl.BlockSpec(memory_space=pltpu.SMEM)] * count


def params(mib):
    return pltpu.CompilerParams(vmem_limit_bytes=mib << 20)


def cost(flops, transcendentals=0, bytes_accessed=1 << 20):
    return pl.CostEstimate(
        flops=flops, transcendentals=transcendentals, bytes_accessed=bytes_accessed
    )


def per_device(
    hidden,
    passage_queries,
    key_weight,
    value_weight,
    decode_queries,
    new_keys,
    new_values,
    cache_keys,
    cache_values,
    cache_lengths,
    passage_of_row,
):
    near, far = tables()
    core, y, s = lax.axis_index("core"), lax.axis_index("y"), lax.axis_index("seq")
    group, groups, ys = lax.axis_index("group"), lax.axis_size("group"), lax.axis_size("y")
    tp = y * 2 + core
    where = jnp.stack([s, core, tp, y, group, s, s, s]).astype(jnp.int32)
    features = hidden.shape[2]
    swap = [(0, 1), (1, 0)]
    state = (32, 2 * HS)

    def call(kernel, out, scalars, arrays, *operands, spaces=(), mib=32, **more):
        single = not isinstance(out, list)
        result = pl.pallas_call(
            kernel,
            in_specs=smem(scalars) + vmem(arrays) + list(spaces),
            out_specs=vmem(1 if single else len(out)),
            out_shape=[out] if single else out,
            compiler_params=params(mib),
            **more,
        )(*operands)
        return result[0] if single else result

    shape = jax.ShapeDtypeStruct
    hbm = pl.BlockSpec(memory_space=pl.ANY)

    with jax.named_scope("projection"):
        width = 2
        block = pl.BlockSpec((width, HALF + EXTRA, 2 * HS), lambda i: (i, 0, 0))
        chunk = shape((KVH, HALF + EXTRA, 2 * HS), bf16)
        mine, theirs = pl.pallas_call(
            project,
            grid=(KVH // width,),
            in_specs=smem(1)
            + [
                pl.BlockSpec((TOK, features), lambda i: (0, 0)),
                pl.BlockSpec((features, width * HS), lambda i: (0, i)),
                pl.BlockSpec((features, width * HS), lambda i: (0, i)),
            ],
            out_specs=[block, block],
            out_shape=[chunk, chunk],
            scratch_shapes=[pltpu.VMEM((2, EXTRA, 256), bf16)],
            compiler_params=params(56),
            cost_estimate=cost(2 * TOK * features * 2048, 0, 4 << 20),
        )(where, hidden[0], key_weight, value_weight)
        theirs = lax.ppermute(theirs, "core", swap)
        chunks = call(add, chunk, 0, 2, mine, theirs, cost_estimate=cost(1 << 20))
        sums = lax.all_to_all(chunks, "y", 0, 0, tiled=True)

    with jax.named_scope("decode_query_exchange"):
        queries = decode_queries.reshape(8, -1).astype(f32)
        own = lax.dynamic_slice_in_dim(queries, tp * HEADS * HS, HEADS * HS, 1)
        near_group = lax.ppermute(own, "group", [(g, g ^ 1) for g in range(groups)])
        far_groups = lax.ppermute(
            jnp.concatenate([own, near_group]), "group", [(g, g ^ 2) for g in range(groups)]
        )

    with jax.named_scope("cache"):
        news = jnp.concatenate([new_keys, new_values], axis=2).reshape(8, -1).astype(f32)
        keep, send = call(
            cache_states,
            [shape((KVH, *state), f32)] * 2,
            2,
            4,
            where,
            cache_lengths,
            queries,
            news,
            cache_keys,
            cache_values,
            cost_estimate=cost(8 * 64 * 256 * 128 * 4, 8 * 64 * 256, 2 << 20),
        )
        other = lax.ppermute(send, "core", swap)
        for bit in (2, 1, 0):
            half = keep.shape[0] // 2
            keep, send = call(
                functools.partial(merge_halves, bit),
                [shape((half, *state), f32)] * 2,
                1,
                2,
                where,
                keep,
                other,
                cost_estimate=cost(1 << 18),
            )
            other = lax.ppermute(send, "y", [(i, i ^ (1 << bit)) for i in range(ys)])
            if bit == 2:
                early = other
        cached = call(
            merge_last, shape((1, *state), f32), 0, 2, keep, other, cost_estimate=cost(1 << 16)
        )

    with jax.named_scope("share"):
        share = call(
            finish_share,
            shape((SEQ, HALF, 2 * HS), bf16),
            1,
            3,
            where,
            sums,
            near,
            far,
            far_groups,
            early,
            spaces=(hbm, hbm),
            cost_estimate=cost(1 << 20),
        )
        received = lax.all_to_all(share, "seq", 0, 0, tiled=True)

    with jax.named_scope("passage_rows"):
        own_kv, _ = lax.optimization_barrier((received.reshape(SEQ * HALF, 2 * HS), cached))
        other_kv = lax.ppermute(own_kv, "core", swap)
        rows_passage = call(
            passage_states,
            shape((groups, *state), f32),
            1,
            5,
            where,
            own,
            near_group,
            far_groups,
            own_kv,
            other_kv,
            cached,
            spaces=(hbm,),
            cost_estimate=cost(128 * 3072 * 128 * 4, 128 * 3072, 2 << 20),
        )
        returned = lax.all_to_all(rows_passage, "group", 0, 0, tiled=True)

    with jax.named_scope("passage_attention"):
        passage_out = call(
            attend,
            shape((TOK, HEADS * HS), bf16),
            1,
            5,
            where,
            passage_queries[0],
            near,
            far,
            own_kv,
            other_kv,
            mib=48,
            scratch_shapes=[
                pltpu.VMEM((HEADS, TOK, HS), f32),
                pltpu.VMEM((HEADS, TOK, 2 * HS), f32),
                pltpu.VMEM((HEADS, TOK, HS), bf16),
            ],
            cost_estimate=cost(1536 * 3072 * 128 * 4 * 4, 1536 * 3072, 3 << 20),
        )

    with jax.named_scope("row_merge"):
        row_out = call(
            merge,
            shape((8, HEADS * HS), f32),
            1,
            2,
            passage_of_row,
            returned,
            cached,
            cost_estimate=cost(1 << 20),
        )
    return passage_out[None], row_out.astype(bf16).reshape(4, 2, HEADS * HS)


def solution(mesh):
    shape = tuple(mesh.shape[name] for name in ("group", "seq", "tp"))
    split = Mesh(
        mesh.devices.reshape(shape[0], shape[1], shape[2] // 2, 2), ("group", "seq", "y", "core")
    )
    tp, rows = ("y", "core"), ("group", "seq")
    in_specs = (
        P("group", "seq", tp),
        P("group", "seq", tp),
        P(tp, None),
        P(tp, None),
        P(None, rows, None),
        P(None, rows, None),
        P(None, rows, None),
        P(rows, tp, None),
        P(rows, tp, None),
        P(rows),
        P(rows),
    )
    out_specs = (P("group", "seq", tp), P(None, rows, tp))
    return jax.shard_map(
        per_device, mesh=split, in_specs=in_specs, out_specs=out_specs, check_vma=False
    )
```

```python
import functools

import jax
import jax.numpy as jnp
import numpy as np
from jax import lax
from jax.experimental import pallas as pl
from jax.experimental.pallas import tpu as pltpu
from jax.sharding import Mesh
from jax.sharding import PartitionSpec as P

D = 8192
KVH = 8
HS = 128
SEQ = 8
TOK = 384
HALF = 192
HEADS = 4
EXTRA = 16
KV_ROWS = HALF + EXTRA
ROWS = KV_ROWS + 32
ROPE_BASE = 500000.0
NORM_EPS = 1e-05
NEG = -1e30
SCALE2 = float(HS**-0.5 * np.log2(np.e))

bf16, f32 = jnp.bfloat16, jnp.float32
dot = functools.partial(jnp.dot, preferred_element_type=f32)


def dot_t(a, b):
    return lax.dot_general(a, b, (((1,), (1,)), ((), ())), preferred_element_type=f32)


def tables():
    freq = ROPE_BASE ** (-(np.arange(HS // 2) * 2.0 / HS))
    freq = np.concatenate([freq, freq])
    near = np.arange(TOK)[:, None] * freq
    far = (np.arange(SEQ) * TOK)[:, None] * freq
    near = np.stack([np.cos(near), np.sin(near)]).astype(np.float32)
    far = np.stack([np.cos(far), np.sin(far)]).astype(np.float32)
    return near, far


def turn_by(near_ref, far_ref, s, rows):
    cn, sn = near_ref[0, rows, :], near_ref[1, rows, :]
    cf, sf = far_ref[0, pl.ds(s, 1), :], far_ref[1, pl.ds(s, 1), :]
    cosine = cn * cf - sn * sf
    sine = sn * cf + cn * sf
    lane = lax.broadcasted_iota(jnp.int32, sine.shape, 1)
    return cosine, jnp.where(lane < HS // 2, -sine, sine)


def turned(x, cosine, sine):
    return x * cosine + pltpu.roll(x, HS // 2, 1) * sine


def project(hidden_ref, key_ref, value_ref, mine_ref, theirs_ref, squares_ref, rows_ref):
    core = lax.axis_index("core")

    @pl.when(pl.program_id(0) == 0)
    def _():
        for half, at in enumerate((core, 1 - core)):
            rows = pl.ds(pl.multiple_of(at * HALF, HALF), HALF)
            rows_ref[half * HALF : (half + 1) * HALF] = hidden_ref[rows, :]
        h = rows_ref[...].astype(f32)
        squares = jnp.broadcast_to(jnp.sum(h * h, axis=1, keepdims=True), (TOK, HS))
        squares = jnp.transpose(squares)[:EXTRA]
        row = lax.broadcasted_iota(jnp.int32, (EXTRA, 256), 0)
        tp = lax.axis_index("y") * 2 + core
        for half in range(2):
            part = squares[:, half * HALF : (half + 1) * HALF]
            part = jnp.concatenate([part, jnp.zeros((EXTRA, 256 - HALF), f32)], axis=1)
            squares_ref[half] = jnp.where(row == tp, part, 0.0).astype(bf16)

    h = rows_ref[...]
    for half, out_ref in enumerate((mine_ref, theirs_ref)):
        for j in range(out_ref.shape[0]):
            out_ref[j, HALF:, :] = squares_ref[half]
    for at, weight_ref in ((0, key_ref), (HS, value_ref)):
        for j in range(0, mine_ref.shape[0], 2):
            both = dot(h, weight_ref[:, j * HS : (j + 2) * HS]).astype(bf16)
            for half, out_ref in enumerate((mine_ref, theirs_ref)):
                part = both[half * HALF : (half + 1) * HALF]
                out_ref[j, :HALF, at : at + HS] = part[:, :HS]
                out_ref[j + 1, :HALF, at : at + HS] = part[:, HS:]


def add(mine_ref, other_ref, cache_ref, tail_ref, out_ref):
    total = mine_ref[...].astype(f32) + other_ref[...].astype(f32)
    out_ref[:, :HALF, :] = total[:, :HALF, :].astype(bf16)
    out_ref[:, HALF:KV_ROWS, :] = (total[:, HALF:, :] + tail_ref[...].astype(f32)).astype(bf16)
    out_ref[:, KV_ROWS:, :] = cache_ref[...]


def finish_share(sums_ref, near_ref, far_ref, out_ref, keep_ref, send_ref):
    s, core = lax.axis_index("seq"), lax.axis_index("core")
    count = sums_ref.shape[0]
    squares, sums, highs, totals = 0.0, 0.0, [], []
    for k in range(count):
        sums = sums + sums_ref[k, :HALF, :].astype(f32)
        extra = sums_ref[k, HALF:KV_ROWS, :].astype(f32)
        squares = squares + extra
        highs.append(extra[0:1, HALF:] + extra[1:2, HALF:] + extra[2:3, HALF:])
        totals.append(extra[3:4, HALF:] + extra[4:5, HALF:] + extra[5:6, HALF:])
    highest = functools.reduce(jnp.maximum, highs)
    factors = [jnp.exp2(high - highest) for high in highs]
    total = sum(f * t for f, t in zip(factors, totals, strict=True))
    rows = lax.broadcasted_iota(jnp.int32, (EXTRA, 256 - HALF), 0)
    table = 0.0
    for i, row in enumerate([*factors, highest, total]):
        table = jnp.where(rows == i, row, table)
    table = jnp.concatenate([table, jnp.zeros((EXTRA, HALF - HS), f32)], axis=1)
    table = jnp.transpose(table)[: 256 - HALF, :]
    weighted = 0.0
    for k in range(count):
        both = sums_ref[k, KV_ROWS:, :].astype(f32)
        both = jnp.concatenate([both[:, :HS], both[:, HS:]], axis=0)
        weighted = weighted + both * table[:, k : k + 1]
    state = state_of(weighted, table[:, count : count + 1], table[:, count + 1 : count + 2])
    keep_ref[...] = jnp.where(core == 0, state[:32], state[32:])
    send_ref[...] = jnp.where(core == 0, state[32:], state[:32])
    squares = jnp.sum(squares, axis=0, keepdims=True)
    inverse = lax.rsqrt(squares * (1.0 / D) + NORM_EPS)
    inverse = jnp.transpose(jnp.broadcast_to(inverse, (8, 256)))[:HALF, 0:1]
    alive = inverse > 0.0
    scaled = jnp.where(alive, sums * inverse, 0.0)
    rows = pl.ds(pl.multiple_of(core * HALF, HALF), HALF)
    cosine, sine = turn_by(near_ref, far_ref, s, rows)
    keys = turned(scaled[:, :HS], cosine, sine)
    share = jnp.concatenate([keys, scaled[:, HS:]], axis=1).astype(bf16)
    for to in range(SEQ):
        out_ref[to] = share


def state_of(weighted, highest, totals):
    lane = lax.broadcasted_iota(jnp.int32, weighted.shape, weighted.ndim - 1)
    tail = jnp.where(lane < HS // 2, highest, totals)
    return jnp.concatenate([weighted, tail], axis=-1)


def parts_of(state):
    return state[..., :HS], state[..., HS : HS + 1], state[..., HS + HS // 2 : HS + HS // 2 + 1]


def merged(a, b):
    (a_sum, a_high, a_total), (b_sum, b_high, b_total) = parts_of(a), parts_of(b)
    highest = jnp.maximum(a_high, b_high)
    a_factor, b_factor = jnp.exp2(a_high - highest), jnp.exp2(b_high - highest)
    return state_of(
        a_sum * a_factor + b_sum * b_factor, highest, a_total * a_factor + b_total * b_factor
    )


def pieces(x):
    first = x.astype(bf16).astype(f32)
    second = (x - first).astype(bf16).astype(f32)
    return first, second, x - first - second


def cache_states(
    length_ref, passage_ref, query_ref, new_ref, key_ref, value_ref, sum_ref, tail_ref, chosen_ref
):
    tp = lax.axis_index("y") * 2 + lax.axis_index("core")
    slots = key_ref.shape[1]
    rows, keys = KVH * 64, 2 * slots + 16
    row = lax.broadcasted_iota(jnp.int32, chosen_ref.shape, 0) & 1
    chosen_ref[...] = jnp.where(row == 1, passage_ref[1], passage_ref[0])

    q = lax.broadcasted_iota(jnp.int32, (64, keys), 0)
    n = lax.broadcasted_iota(jnp.int32, (64, keys), 1)
    key_row = jnp.where(n >= slots, 1, 0)
    slot = tp * slots + n - key_row * slots
    length = jnp.where(key_row == 1, length_ref[1], length_ref[0])
    live = ((q & 1) == key_row) & (slot < length) & (n < 2 * slots)
    new = n - 2 * slots
    recent = ((q & 1) == (new & 1)) & ((new >> 1) <= ((q & 7) >> 1)) & (tp == 0)
    live = live | (recent & (new >= 0) & (new < 8))
    live = jnp.where(live, 1.0, 0.0)
    live = jnp.concatenate([live] * KVH, axis=0) > 0.5

    news = jnp.concatenate([new_ref[...], jnp.zeros(new_ref.shape, f32)], axis=0).astype(bf16)
    scores = []
    for head in range(KVH):
        cols = slice(head * HS, (head + 1) * HS)
        query = jnp.concatenate(
            [query_ref[:, (head * 8 + p) * HS : (head * 8 + p + 1) * HS] for p in range(8)], axis=0
        ).astype(bf16)
        every = jnp.concatenate([key_ref[0, :, cols], key_ref[1, :, cols], news[:, cols]], axis=0)
        scores.append(dot_t(query, every))
    scores = jnp.where(live, jnp.concatenate(scores, axis=0) * SCALE2, NEG)
    highest = jnp.max(scores, axis=1, keepdims=True)
    weights = jnp.where(live, jnp.exp2(scores - highest), 0.0)
    totals = jnp.sum(weights, axis=1, keepdims=True)
    weights = weights.astype(bf16)
    lane = lax.broadcasted_iota(jnp.int32, (rows, HS), 1)
    tail = 0.0
    for i, piece in enumerate(pieces(highest) + pieces(totals)):
        tail = jnp.where(lane == i, piece, tail)
    tail = jnp.transpose(tail)[:EXTRA, :]
    for head in range(KVH):
        cols = slice(head * HS, (head + 1) * HS)
        part = slice(head * 64, (head + 1) * 64)
        late = slice((KVH + head) * HS, (KVH + head + 1) * HS)
        every = jnp.concatenate(
            [value_ref[0, :, cols], value_ref[1, :, cols], news[:, late]], axis=0
        )
        weighted = dot(weights[part], every)
        sum_ref[head] = jnp.concatenate([weighted[:32], weighted[32:]], axis=1).astype(bf16)
        tail_ref[head] = jnp.concatenate(
            [jnp.zeros((EXTRA, HALF), f32), tail[:, part]], axis=1
        ).astype(bf16)


def passage_states(
    query_ref, query1_ref, query2_ref, own_ref, other_ref, out_ref
):
    queries = [query_ref[...], query1_ref[...], query2_ref[:8, :], query2_ref[8:, :]]
    query = jnp.concatenate(
        [rows[:, p * HS : (p + 1) * HS] for rows in queries for p in range(HEADS)], axis=0
    ).astype(bf16)
    refs = (own_ref, other_ref)
    scores = [dot_t(query, ref[:, :HS]) * SCALE2 for ref in refs]
    highest = jnp.max(jnp.maximum(*scores), axis=1, keepdims=True)
    weights = [jnp.exp2(score - highest) for score in scores]
    totals = jnp.sum(weights[0] + weights[1], axis=1, keepdims=True)
    weighted = sum(dot(w.astype(bf16), ref[:, HS:]) for w, ref in zip(weights, refs, strict=True))
    state = state_of(weighted, highest, totals)
    for r in range(4):
        out_ref[lax.axis_index("group") ^ r] = state[32 * r : 32 * (r + 1)]


def attend(query_ref, near_ref, far_ref, own_ref, other_ref, out_ref, turned_ref, values_ref):
    s, core = lax.axis_index("seq"), lax.axis_index("core")
    cosine, sine = turn_by(near_ref, far_ref, s, slice(None))
    cosine, sine = cosine * SCALE2, sine * SCALE2
    for h in range(HEADS):
        x = query_ref[:, h * HS : (h + 1) * HS].astype(f32)
        turned_ref[h] = turned(x, cosine, sine).astype(bf16)

    def run(pairs):
        keys = pairs * TOK
        early, late = slice(0, keys - TOK), slice(keys - TOK, keys)
        for c, ref in enumerate((own_ref, other_ref)):
            values_ref[c, :keys, :HS] = ref[:keys, HS:]
            values_ref[c, :keys, HS:] = jnp.ones((keys, HS), bf16)
        n = lax.broadcasted_iota(jnp.int32, (1, TOK), 1)
        second = jnp.where(n >= HALF, 1, 0)
        key_pos = (2 * (pairs - 1) + second) * TOK + n - second * HALF
        query_pos = s * TOK + lax.broadcasted_iota(jnp.int32, (TOK, 1), 0)

        def head(h, carry):
            query = turned_ref[h]
            scores, values = [], []
            for c, ref in enumerate((own_ref, other_ref)):
                if pairs > 1:
                    scores.append(dot_t(query, ref[early, :HS]))
                    values.append(values_ref[c, early, :])
                offset = core * HALF if c == 0 else (1 - core) * HALF
                score = dot_t(query, ref[late, :HS])
                scores.append(jnp.where(key_pos + offset <= query_pos, score, NEG))
                values.append(values_ref[c, late, :])
            highest = functools.reduce(
                jnp.maximum, [jnp.max(score, axis=1, keepdims=True) for score in scores]
            )
            total = 0.0
            for score, value in zip(scores, values, strict=True):
                total = total + dot(jnp.exp2(score - highest).astype(bf16), value)
            context = (total[:, :HS] / total[:, HS : HS + 1]).astype(bf16)
            out_ref[:, pl.ds(pl.multiple_of(h * HS, HS), HS)] = context
            return carry

        lax.fori_loop(0, HEADS, head, 0, unroll=2)

    for pairs in range(1, SEQ // 2 + 1):
        pl.when(s // 2 == pairs - 1)(functools.partial(run, pairs))


def merge(chosen_ref, passages_ref, cache_ref, other_ref, out_ref):
    chosen = chosen_ref[...]
    state = passages_ref[0]
    for g in range(1, passages_ref.shape[0]):
        state = jnp.where(chosen == g, passages_ref[g], state)
    weighted, _, total = parts_of(merged(state, merged(cache_ref[...], other_ref[...])))
    context = weighted / total
    for step in range(out_ref.shape[0]):
        for p in range(HEADS):
            rows = context[p * 8 + 2 * step : p * 8 + 2 * step + 2, :]
            out_ref[step, :, p * HS : (p + 1) * HS] = rows.astype(bf16)


def vmem(count):
    return [pl.BlockSpec(memory_space=pltpu.VMEM)] * count


def smem(count):
    return [pl.BlockSpec(memory_space=pltpu.SMEM)] * count


def params(mib):
    return pltpu.CompilerParams(vmem_limit_bytes=mib << 20)


def cost(flops, transcendentals=0, bytes_accessed=1 << 20):
    return pl.CostEstimate(
        flops=flops, transcendentals=transcendentals, bytes_accessed=bytes_accessed
    )


def per_device(
    hidden,
    passage_queries,
    key_weight,
    value_weight,
    decode_queries,
    new_keys,
    new_values,
    cache_keys,
    cache_values,
    cache_lengths,
    passage_of_row,
):
    near, far = tables()
    groups = lax.axis_size("group")
    tp = lax.axis_index("y") * 2 + lax.axis_index("core")
    features = hidden.shape[2]
    swap = [(0, 1), (1, 0)]
    state = (32, 2 * HS)

    def call(kernel, out, scalars, arrays, *operands, mib=32, **more):
        single = not isinstance(out, list)
        result = pl.pallas_call(
            kernel,
            in_specs=smem(scalars) + vmem(arrays),
            out_specs=vmem(1 if single else len(out)),
            out_shape=[out] if single else out,
            compiler_params=params(mib),
            **more,
        )(*operands)
        return result[0] if single else result

    shape = jax.ShapeDtypeStruct

    with jax.named_scope("projection"):
        width = 4
        block = pl.BlockSpec((width, HALF + EXTRA, 2 * HS), lambda i: (i, 0, 0))
        chunk = shape((KVH, HALF + EXTRA, 2 * HS), bf16)
        mine, theirs = pl.pallas_call(
            project,
            grid=(KVH // width,),
            in_specs=[
                pl.BlockSpec((TOK, features), lambda i: (0, 0)),
                pl.BlockSpec((features, width * HS), lambda i: (0, i)),
                pl.BlockSpec((features, width * HS), lambda i: (0, i)),
            ],
            out_specs=[block, block],
            out_shape=[chunk, chunk],
            scratch_shapes=[
                pltpu.VMEM((2, EXTRA, 256), bf16),
                pltpu.VMEM((TOK, features), bf16),
            ],
            compiler_params=params(56),
            cost_estimate=cost(2 * TOK * features * 2048, 0, 4 << 20),
        )(hidden[0], key_weight, value_weight)
        theirs = lax.ppermute(theirs, "core", swap)

    with jax.named_scope("cache"):
        queries = decode_queries.reshape(8, -1).astype(f32)
        news = jnp.concatenate([new_keys, new_values], axis=2).reshape(8, -1).astype(f32)
        cache_sums, cache_tails, chosen = call(
            cache_states,
            [
                shape((KVH, 32, 2 * HS), bf16),
                shape((KVH, EXTRA, 2 * HS), bf16),
                shape(state, jnp.int32),
            ],
            2,
            4,
            cache_lengths,
            passage_of_row,
            queries,
            news,
            cache_keys,
            cache_values,
            cost_estimate=cost(8 * 64 * 256 * 128 * 4, 8 * 64 * 256, 2 << 20),
        )

    with jax.named_scope("sums"):
        chunks = call(
            add,
            shape((KVH, ROWS, 2 * HS), bf16),
            0,
            4,
            mine,
            theirs,
            cache_sums,
            cache_tails,
            cost_estimate=cost(1 << 20),
        )
        sums = lax.all_to_all(chunks, "y", 0, 0, tiled=True)

    with jax.named_scope("decode_query_exchange"):
        queries, _ = lax.optimization_barrier((queries, chunks))
        own = lax.dynamic_slice_in_dim(queries, tp * HEADS * HS, HEADS * HS, 1)
        near_group = lax.ppermute(own, "group", [(g, g ^ 1) for g in range(groups)])
        far_groups = lax.ppermute(
            jnp.concatenate([own, near_group]), "group", [(g, g ^ 2) for g in range(groups)]
        )

    with jax.named_scope("share"):
        sums, far_groups = lax.optimization_barrier((sums, far_groups))
        share, keep, send = call(
            finish_share,
            [shape((SEQ, HALF, 2 * HS), bf16), shape(state, f32), shape(state, f32)],
            0,
            3,
            sums,
            near,
            far,
            cost_estimate=cost(1 << 20),
        )
        received = lax.all_to_all(share, "seq", 0, 0, tiled=True)
        other = lax.ppermute(send, "core", swap)

    with jax.named_scope("passage_rows"):
        own_kv, _ = lax.optimization_barrier((received.reshape(SEQ * HALF, 2 * HS), other))
        other_kv = lax.ppermute(own_kv, "core", swap)
        rows_passage = call(
            passage_states,
            shape((groups, *state), f32),
            0,
            5,
            own,
            near_group,
            far_groups,
            own_kv,
            other_kv,
            cost_estimate=cost(128 * 3072 * 128 * 4, 128 * 3072, 2 << 20),
        )
        returned = lax.all_to_all(rows_passage, "group", 0, 0, tiled=True)

    with jax.named_scope("passage_attention"):
        passage_out = call(
            attend,
            shape((TOK, HEADS * HS), bf16),
            0,
            5,
            passage_queries[0],
            near,
            far,
            own_kv,
            other_kv,
            mib=48,
            scratch_shapes=[
                pltpu.VMEM((HEADS, TOK, HS), bf16),
                pltpu.VMEM((2, SEQ * HALF, 2 * HS), bf16),
            ],
            cost_estimate=cost(1536 * 3072 * 128 * 4 * 4, 1536 * 3072, 3 << 20),
        )

    with jax.named_scope("row_merge"):
        row_out = call(
            merge,
            shape((4, 2, HEADS * HS), bf16),
            0,
            4,
            chosen,
            returned,
            keep,
            other,
            cost_estimate=cost(1 << 20),
        )
    return passage_out[None], row_out


def solution(mesh):
    shape = tuple(mesh.shape[name] for name in ("group", "seq", "tp"))
    split = Mesh(
        mesh.devices.reshape(shape[0], shape[1], shape[2] // 2, 2), ("group", "seq", "y", "core")
    )
    tp, rows = ("y", "core"), ("group", "seq")
    in_specs = (
        P("group", "seq", tp),
        P("group", "seq", tp),
        P(tp, None),
        P(tp, None),
        P(None, rows, None),
        P(None, rows, None),
        P(None, rows, None),
        P(rows, tp, None),
        P(rows, tp, None),
        P(rows),
        P(rows),
    )
    out_specs = (P("group", "seq", tp), P(None, rows, tp))
    return jax.shard_map(
        per_device, mesh=split, in_specs=in_specs, out_specs=out_specs, check_vma=False
    )
```

```python
import functools

import jax
import jax.numpy as jnp
import numpy as np
from jax import lax
from jax.experimental import pallas as pl
from jax.experimental.pallas import tpu as pltpu
from jax.sharding import Mesh
from jax.sharding import PartitionSpec as P

D = 8192
KVH = 8
HS = 128
SEQ = 8
TOK = 384
HALF = 192
HEADS = 4
EXTRA = 16
KV_ROWS = HALF + EXTRA
ROWS = KV_ROWS + 32
ROPE_BASE = 500000.0
NORM_EPS = 1e-05
NEG = -1e30
SCALE2 = float(HS**-0.5 * np.log2(np.e))

bf16, f32 = jnp.bfloat16, jnp.float32
dot = functools.partial(jnp.dot, preferred_element_type=f32)


def dot_t(a, b):
    return lax.dot_general(a, b, (((1,), (1,)), ((), ())), preferred_element_type=f32)


def tables():
    freq = ROPE_BASE ** (-(np.arange(HS // 2) * 2.0 / HS))
    freq = np.concatenate([freq, freq])
    near = np.arange(TOK)[:, None] * freq
    far = (np.arange(SEQ) * TOK)[:, None] * freq
    near = np.stack([np.cos(near), np.sin(near)]).astype(np.float32)
    far = np.stack([np.cos(far), np.sin(far)]).astype(np.float32)
    return near, far


def turn_by(near_ref, far_ref, s, rows):
    cn, sn = near_ref[0, rows, :], near_ref[1, rows, :]
    cf, sf = far_ref[0, pl.ds(s, 1), :], far_ref[1, pl.ds(s, 1), :]
    cosine = cn * cf - sn * sf
    sine = sn * cf + cn * sf
    lane = lax.broadcasted_iota(jnp.int32, sine.shape, 1)
    return cosine, jnp.where(lane < HS // 2, -sine, sine)


def turned(x, cosine, sine):
    return x * cosine + pltpu.roll(x, HS // 2, 1) * sine


def project(hidden_ref, key_ref, value_ref, mine_ref, theirs_ref, squares_ref, rows_ref):
    core = lax.axis_index("core")

    @pl.when(pl.program_id(0) == 0)
    def _():
        for half, at in enumerate((core, 1 - core)):
            rows = pl.ds(pl.multiple_of(at * HALF, HALF), HALF)
            rows_ref[half * HALF : (half + 1) * HALF] = hidden_ref[rows, :]
        h = rows_ref[...].astype(f32)
        squares = jnp.broadcast_to(jnp.sum(h * h, axis=1, keepdims=True), (TOK, HS))
        squares = jnp.transpose(squares)[:EXTRA]
        row = lax.broadcasted_iota(jnp.int32, (EXTRA, 256), 0)
        tp = lax.axis_index("y") * 2 + core
        for half in range(2):
            part = squares[:, half * HALF : (half + 1) * HALF]
            part = jnp.concatenate([part, jnp.zeros((EXTRA, 256 - HALF), f32)], axis=1)
            squares_ref[half] = jnp.where(row == tp, part, 0.0).astype(bf16)

    h = rows_ref[...]
    for half, out_ref in enumerate((mine_ref, theirs_ref)):
        for j in range(out_ref.shape[0]):
            out_ref[j, HALF:, :] = squares_ref[half]
    for at, weight_ref in ((0, key_ref), (HS, value_ref)):
        for j in range(0, mine_ref.shape[0], 2):
            both = dot(h, weight_ref[:, j * HS : (j + 2) * HS]).astype(bf16)
            for half, out_ref in enumerate((mine_ref, theirs_ref)):
                part = both[half * HALF : (half + 1) * HALF]
                out_ref[j, :HALF, at : at + HS] = part[:, :HS]
                out_ref[j + 1, :HALF, at : at + HS] = part[:, HS:]


def add(mine_ref, other_ref, cache_ref, tail_ref, out_ref):
    total = mine_ref[...].astype(f32) + other_ref[...].astype(f32)
    out_ref[:, :HALF, :] = total[:, :HALF, :].astype(bf16)
    out_ref[:, HALF:KV_ROWS, :] = (total[:, HALF:, :] + tail_ref[...].astype(f32)).astype(bf16)
    out_ref[:, KV_ROWS:, :] = cache_ref[...]


def finish_share(sums_ref, near_ref, far_ref, out_ref, keep_ref, send_ref):
    s, core = lax.axis_index("seq"), lax.axis_index("core")
    count = sums_ref.shape[0]
    squares, sums, highs, totals = 0.0, 0.0, [], []
    for k in range(count):
        sums = sums + sums_ref[k, :HALF, :].astype(f32)
        extra = sums_ref[k, HALF:KV_ROWS, :].astype(f32)
        squares = squares + extra
        highs.append(extra[0:1, HALF:] + extra[1:2, HALF:] + extra[2:3, HALF:])
        totals.append(extra[3:4, HALF:] + extra[4:5, HALF:] + extra[5:6, HALF:])
    highest = functools.reduce(jnp.maximum, highs)
    factors = [jnp.exp2(high - highest) for high in highs]
    total = sum(f * t for f, t in zip(factors, totals, strict=True))
    rows = lax.broadcasted_iota(jnp.int32, (EXTRA, 256 - HALF), 0)
    table = 0.0
    for i, row in enumerate([*factors, highest, total]):
        table = jnp.where(rows == i, row, table)
    table = jnp.concatenate([table, jnp.zeros((EXTRA, HALF - HS), f32)], axis=1)
    table = jnp.transpose(table)[: 256 - HALF, :]
    weighted = 0.0
    for k in range(count):
        both = sums_ref[k, KV_ROWS:, :].astype(f32)
        both = jnp.concatenate([both[:, :HS], both[:, HS:]], axis=0)
        weighted = weighted + both * table[:, k : k + 1]
    state = state_of(weighted, table[:, count : count + 1], table[:, count + 1 : count + 2])
    keep_ref[...] = jnp.where(core == 0, state[:32], state[32:])
    send_ref[...] = jnp.where(core == 0, state[32:], state[:32])
    squares = jnp.sum(squares, axis=0, keepdims=True)
    inverse = lax.rsqrt(squares * (1.0 / D) + NORM_EPS)
    inverse = jnp.transpose(jnp.broadcast_to(inverse, (8, 256)))[:HALF, 0:1]
    alive = inverse > 0.0
    scaled = jnp.where(alive, sums * inverse, 0.0)
    rows = pl.ds(pl.multiple_of(core * HALF, HALF), HALF)
    cosine, sine = turn_by(near_ref, far_ref, s, rows)
    keys = turned(scaled[:, :HS], cosine, sine)
    share = jnp.concatenate([keys, scaled[:, HS:]], axis=1).astype(bf16)
    for to in range(SEQ):
        out_ref[to] = share


def state_of(weighted, highest, totals):
    lane = lax.broadcasted_iota(jnp.int32, weighted.shape, weighted.ndim - 1)
    tail = jnp.where(lane < HS // 2, highest, totals)
    return jnp.concatenate([weighted, tail], axis=-1)


def parts_of(state):
    return state[..., :HS], state[..., HS : HS + 1], state[..., HS + HS // 2 : HS + HS // 2 + 1]


def merged(a, b):
    (a_sum, a_high, a_total), (b_sum, b_high, b_total) = parts_of(a), parts_of(b)
    highest = jnp.maximum(a_high, b_high)
    a_factor, b_factor = jnp.exp2(a_high - highest), jnp.exp2(b_high - highest)
    return state_of(
        a_sum * a_factor + b_sum * b_factor, highest, a_total * a_factor + b_total * b_factor
    )


def pieces(x):
    first = x.astype(bf16).astype(f32)
    second = (x - first).astype(bf16).astype(f32)
    return first, second, x - first - second


def cache_states(
    length_ref, passage_ref, query_ref, new_ref, key_ref, value_ref, sum_ref, tail_ref, chosen_ref
):
    tp = lax.axis_index("y") * 2 + lax.axis_index("core")
    slots = key_ref.shape[1]
    rows, keys = KVH * 64, 2 * slots + 16
    row = lax.broadcasted_iota(jnp.int32, chosen_ref.shape, 0) & 1
    chosen_ref[...] = jnp.where(row == 1, passage_ref[1], passage_ref[0])

    q = lax.broadcasted_iota(jnp.int32, (64, keys), 0)
    n = lax.broadcasted_iota(jnp.int32, (64, keys), 1)
    key_row = jnp.where(n >= slots, 1, 0)
    slot = tp * slots + n - key_row * slots
    length = jnp.where(key_row == 1, length_ref[1], length_ref[0])
    live = ((q & 1) == key_row) & (slot < length) & (n < 2 * slots)
    new = n - 2 * slots
    recent = ((q & 1) == (new & 1)) & ((new >> 1) <= ((q & 7) >> 1)) & (tp == 0)
    live = live | (recent & (new >= 0) & (new < 8))
    live = jnp.where(live, 1.0, 0.0)
    live = jnp.concatenate([live] * KVH, axis=0) > 0.5

    news = jnp.concatenate([new_ref[...], jnp.zeros(new_ref.shape, f32)], axis=0).astype(bf16)
    scores = []
    for head in range(KVH):
        cols = slice(head * HS, (head + 1) * HS)
        query = jnp.concatenate(
            [query_ref[:, (head * 8 + p) * HS : (head * 8 + p + 1) * HS] for p in range(8)], axis=0
        ).astype(bf16)
        every = jnp.concatenate([key_ref[0, :, cols], key_ref[1, :, cols], news[:, cols]], axis=0)
        scores.append(dot_t(query, every))
    scores = jnp.where(live, jnp.concatenate(scores, axis=0) * SCALE2, NEG)
    highest = jnp.max(scores, axis=1, keepdims=True)
    weights = jnp.where(live, jnp.exp2(scores - highest), 0.0)
    totals = jnp.sum(weights, axis=1, keepdims=True)
    weights = weights.astype(bf16)
    lane = lax.broadcasted_iota(jnp.int32, (rows, HS), 1)
    tail = 0.0
    for i, piece in enumerate(pieces(highest) + pieces(totals)):
        tail = jnp.where(lane == i, piece, tail)
    tail = jnp.transpose(tail)[:EXTRA, :]
    for head in range(KVH):
        cols = slice(head * HS, (head + 1) * HS)
        part = slice(head * 64, (head + 1) * 64)
        late = slice((KVH + head) * HS, (KVH + head + 1) * HS)
        every = jnp.concatenate(
            [value_ref[0, :, cols], value_ref[1, :, cols], news[:, late]], axis=0
        )
        weighted = dot(weights[part], every)
        sum_ref[head] = jnp.concatenate([weighted[:32], weighted[32:]], axis=1).astype(bf16)
        tail_ref[head] = jnp.concatenate(
            [jnp.zeros((EXTRA, HALF), f32), tail[:, part]], axis=1
        ).astype(bf16)


def passage_states(query_ref, query1_ref, query2_ref, kv_ref, out_ref):
    heads = 2 * HEADS
    queries = [query_ref[...], query1_ref[...], query2_ref[:8, :], query2_ref[8:, :]]
    query = jnp.concatenate(
        [rows[:, p * HS : (p + 1) * HS] for rows in queries for p in range(heads)], axis=0
    ).astype(bf16)
    scores = dot_t(query, kv_ref[:, :HS]) * SCALE2
    highest = jnp.max(scores, axis=1, keepdims=True)
    weights = jnp.exp2(scores - highest)
    totals = jnp.sum(weights, axis=1, keepdims=True)
    weighted = dot(weights.astype(bf16), kv_ref[:, HS:])
    state = state_of(weighted, highest, totals)
    for r in range(4):
        for core in range(2):
            at = (2 * r + core) * 32
            out_ref[2 * (lax.axis_index("group") ^ r) + core] = state[at : at + 32]


def turn_queries(query_ref, near_ref, far_ref, out_ref):
    cosine, sine = turn_by(near_ref, far_ref, lax.axis_index("seq"), slice(None))
    cosine, sine = cosine * SCALE2, sine * SCALE2
    for h in range(HEADS):
        x = query_ref[:, h * HS : (h + 1) * HS].astype(f32)
        out_ref[h] = turned(x, cosine, sine).astype(bf16)


def attend(turned_ref, own_ref, other_ref, out_ref, values_ref):
    s, core = lax.axis_index("seq"), lax.axis_index("core")

    def run(pairs):
        keys = pairs * TOK
        early, late = slice(0, keys - TOK), slice(keys - TOK, keys)
        for c, ref in enumerate((own_ref, other_ref)):
            values_ref[c, :keys, :HS] = ref[:keys, HS:]
            values_ref[c, :keys, HS:] = jnp.ones((keys, HS), bf16)
        n = lax.broadcasted_iota(jnp.int32, (1, TOK), 1)
        second = jnp.where(n >= HALF, 1, 0)
        key_pos = (2 * (pairs - 1) + second) * TOK + n - second * HALF
        query_pos = s * TOK + lax.broadcasted_iota(jnp.int32, (TOK, 1), 0)

        def head(h, carry):
            query = turned_ref[h]
            scores, values = [], []
            for c, ref in enumerate((own_ref, other_ref)):
                if pairs > 1:
                    scores.append(dot_t(query, ref[early, :HS]))
                    values.append(values_ref[c, early, :])
                offset = core * HALF if c == 0 else (1 - core) * HALF
                score = dot_t(query, ref[late, :HS])
                scores.append(jnp.where(key_pos + offset <= query_pos, score, NEG))
                values.append(values_ref[c, late, :])
            highest = functools.reduce(
                jnp.maximum, [jnp.max(score, axis=1, keepdims=True) for score in scores]
            )
            total = 0.0
            for score, value in zip(scores, values, strict=True):
                total = total + dot(jnp.exp2(score - highest).astype(bf16), value)
            context = (total[:, :HS] / total[:, HS : HS + 1]).astype(bf16)
            out_ref[:, pl.ds(pl.multiple_of(h * HS, HS), HS)] = context
            return carry

        lax.fori_loop(0, HEADS, head, 0, unroll=2)

    for pairs in range(1, SEQ // 2 + 1):
        pl.when(s // 2 == pairs - 1)(functools.partial(run, pairs))


def merge(chosen_ref, passages_ref, cache_ref, other_ref, out_ref):
    chosen = chosen_ref[...]
    states = [passages_ref[0], passages_ref[1]]
    for g in range(1, passages_ref.shape[0] // 2):
        for core in range(2):
            states[core] = jnp.where(chosen == g, passages_ref[2 * g + core], states[core])
    states += [cache_ref[...], other_ref[...]]
    weighted, _, total = parts_of(merged(merged(*states[:2]), merged(*states[2:])))
    context = weighted / total
    for step in range(out_ref.shape[0]):
        for p in range(HEADS):
            rows = context[p * 8 + 2 * step : p * 8 + 2 * step + 2, :]
            out_ref[step, :, p * HS : (p + 1) * HS] = rows.astype(bf16)


def vmem(count):
    return [pl.BlockSpec(memory_space=pltpu.VMEM)] * count


def smem(count):
    return [pl.BlockSpec(memory_space=pltpu.SMEM)] * count


def params(mib):
    return pltpu.CompilerParams(vmem_limit_bytes=mib << 20)


def cost(flops, transcendentals=0, bytes_accessed=1 << 20):
    return pl.CostEstimate(
        flops=flops, transcendentals=transcendentals, bytes_accessed=bytes_accessed
    )


def per_device(
    hidden,
    passage_queries,
    key_weight,
    value_weight,
    decode_queries,
    new_keys,
    new_values,
    cache_keys,
    cache_values,
    cache_lengths,
    passage_of_row,
):
    near, far = tables()
    groups = lax.axis_size("group")
    features = hidden.shape[2]
    swap = [(0, 1), (1, 0)]
    state = (32, 2 * HS)

    def call(kernel, out, scalars, arrays, *operands, mib=32, **more):
        single = not isinstance(out, list)
        result = pl.pallas_call(
            kernel,
            in_specs=smem(scalars) + vmem(arrays),
            out_specs=vmem(1 if single else len(out)),
            out_shape=[out] if single else out,
            compiler_params=params(mib),
            **more,
        )(*operands)
        return result[0] if single else result

    shape = jax.ShapeDtypeStruct

    with jax.named_scope("projection"):
        width = 4
        block = pl.BlockSpec((width, HALF + EXTRA, 2 * HS), lambda i: (i, 0, 0))
        chunk = shape((KVH, HALF + EXTRA, 2 * HS), bf16)
        mine, theirs = pl.pallas_call(
            project,
            grid=(KVH // width,),
            in_specs=[
                pl.BlockSpec((TOK, features), lambda i: (0, 0)),
                pl.BlockSpec((features, width * HS), lambda i: (0, i)),
                pl.BlockSpec((features, width * HS), lambda i: (0, i)),
            ],
            out_specs=[block, block],
            out_shape=[chunk, chunk],
            scratch_shapes=[
                pltpu.VMEM((2, EXTRA, 256), bf16),
                pltpu.VMEM((TOK, features), bf16),
            ],
            compiler_params=params(56),
            cost_estimate=cost(2 * TOK * features * 2048, 0, 4 << 20),
        )(hidden[0], key_weight, value_weight)
        theirs = lax.ppermute(theirs, "core", swap)

    with jax.named_scope("cache"):
        queries = decode_queries.reshape(8, -1).astype(f32)
        news = jnp.concatenate([new_keys, new_values], axis=2).reshape(8, -1).astype(f32)
        cache_sums, cache_tails, chosen = call(
            cache_states,
            [
                shape((KVH, 32, 2 * HS), bf16),
                shape((KVH, EXTRA, 2 * HS), bf16),
                shape(state, jnp.int32),
            ],
            2,
            4,
            cache_lengths,
            passage_of_row,
            queries,
            news,
            cache_keys,
            cache_values,
            cost_estimate=cost(8 * 64 * 256 * 128 * 4, 8 * 64 * 256, 2 << 20),
        )

    with jax.named_scope("sums"):
        chunks = call(
            add,
            shape((KVH, ROWS, 2 * HS), bf16),
            0,
            4,
            mine,
            theirs,
            cache_sums,
            cache_tails,
            cost_estimate=cost(1 << 20),
        )
        sums = lax.all_to_all(chunks, "y", 0, 0, tiled=True)

    with jax.named_scope("decode_query_exchange"):
        queries, _ = lax.optimization_barrier((queries, chunks))
        own = lax.dynamic_slice_in_dim(queries, lax.axis_index("y") * 8 * HS, 8 * HS, 1)
        near_group = lax.ppermute(own, "group", [(g, g ^ 1) for g in range(groups)])
        far_groups = lax.ppermute(
            jnp.concatenate([own, near_group]), "group", [(g, g ^ 2) for g in range(groups)]
        )

    with jax.named_scope("share"):
        queries, _ = lax.optimization_barrier((passage_queries[0], chunks))
        turned_queries = call(
            turn_queries,
            shape((HEADS, TOK, HS), bf16),
            0,
            3,
            queries,
            near,
            far,
            cost_estimate=cost(1 << 20),
        )
        sums, far_groups, turned_queries = lax.optimization_barrier(
            (sums, far_groups, turned_queries)
        )
        share, keep, send = call(
            finish_share,
            [shape((SEQ, HALF, 2 * HS), bf16), shape(state, f32), shape(state, f32)],
            0,
            3,
            sums,
            near,
            far,
            cost_estimate=cost(1 << 20),
        )
        received = lax.all_to_all(share, "seq", 0, 0, tiled=True)
        other = lax.ppermute(send, "core", swap)

    with jax.named_scope("passage_rows"):
        own_kv, _ = lax.optimization_barrier((received.reshape(SEQ * HALF, 2 * HS), other))
        other_kv = lax.ppermute(own_kv, "core", swap)
        rows_passage = call(
            passage_states,
            shape((2 * groups, *state), f32),
            0,
            4,
            own,
            near_group,
            far_groups,
            own_kv,
            cost_estimate=cost(256 * 1536 * 128 * 4, 256 * 1536, 2 << 20),
        )
        returned = lax.all_to_all(rows_passage, ("group", "core"), 0, 0, tiled=True)

    with jax.named_scope("passage_attention"):
        passage_out = call(
            attend,
            shape((TOK, HEADS * HS), bf16),
            0,
            3,
            turned_queries,
            own_kv,
            other_kv,
            mib=48,
            scratch_shapes=[pltpu.VMEM((2, SEQ * HALF, 2 * HS), bf16)],
            cost_estimate=cost(1536 * 3072 * 128 * 4 * 4, 1536 * 3072, 3 << 20),
        )

    with jax.named_scope("row_merge"):
        chosen, passage_out = lax.optimization_barrier((chosen, passage_out))
        row_out = call(
            merge,
            shape((4, 2, HEADS * HS), bf16),
            0,
            4,
            chosen,
            returned,
            keep,
            other,
            cost_estimate=cost(1 << 20),
        )
    return passage_out[None], row_out


def solution(mesh):
    shape = tuple(mesh.shape[name] for name in ("group", "seq", "tp"))
    split = Mesh(
        mesh.devices.reshape(shape[0], shape[1], shape[2] // 2, 2), ("group", "seq", "y", "core")
    )
    tp, rows = ("y", "core"), ("group", "seq")
    in_specs = (
        P("group", "seq", tp),
        P("group", "seq", tp),
        P(tp, None),
        P(tp, None),
        P(None, rows, None),
        P(None, rows, None),
        P(None, rows, None),
        P(rows, tp, None),
        P(rows, tp, None),
        P(rows),
        P(rows),
    )
    out_specs = (P("group", "seq", tp), P(None, rows, tp))
    return jax.shard_map(
        per_device, mesh=split, in_specs=in_specs, out_specs=out_specs, check_vma=False
    )
```
